32 devices in a mesh: groups: 2 (over y), dp: 4 (over z), mp: 2 (over x), sub: 2 (over core).
Axes of the slice: x: 2, y: 2, z: 4, core: 2. Of those that a mesh axis runs over, the one named last changes fastest.
Arguments:
- upstream: bfloat16 [4096, 4096], P(('groups', 'dp')), parts along dimension 0, may hold values from -6 to 6
- attn: bfloat16 [4096, 4096], P(('groups', 'dp'), ('mp', 'sub')), parts along dimension 0, may hold values from -6 to 6
- gate: bfloat16 [8, 4096], P(('groups', 'dp')), parts along dimension 0, may hold values from -4 to 4
- visible: int32 [8], P(('groups', 'dp')), parts along dimension 0, may hold values from 1 to 3, as said below
- proj_weight: bfloat16 [4096, 4096], P(('mp', 'sub'), 'dp'), may hold values from -0.09375 to 0.09375
Outputs:
- grad_attn: bfloat16 [4096, 4096], P(('groups', 'dp'), ('mp', 'sub')), parts along dimension 0
- grad_weight: bfloat16 [4096, 8192], P(('mp', 'sub'), ('groups', 'dp')), parts along dimension 1
The draws below stay inside these ranges and needn't reach their ends.
There are 2 independent parts, one for each index of `groups`. The reference program is written for one: setup_inputs(seed, part) draws one part's arguments, and reference() takes and returns one part's arrays. A program takes and returns all parts, laid end to end along the dimension named above; an argument that names none is the same for every part. Nothing has to cross between parts.
Inputs may be any that keep to these rules, and one draw needn't show every extreme that they name: Images i and i + 4 / 2 (for i below 2) have at most 4 visible blocks together; some image has exactly 3.
All inputs are finite; a program needn't handle non-finite values.
Results may differ from the reference program's by a relative error of at most 0.005.
Values may be sent and summed in bfloat16 or wider, within the bound.
A program may use at most 128 MiB of HBM per device.

```python
import jax
import jax.numpy as jnp

D = 4096
BLOCK = 128
CAP = 512
ROWS = 2048
N_DP = 4


def draw_visible(key, part):
    key = jax.random.fold_in(key, 7)
    half = N_DP // 2
    key_kind, key_force, key_side = jax.random.split(key, 3)
    first_table = jnp.array([1, 1, 2, 1, 3, 2], dtype=jnp.int32)
    second_table = jnp.array([1, 2, 1, 3, 1, 2], dtype=jnp.int32)
    kinds = jax.random.randint(key_kind, (half,), 0, 6).astype(jnp.int32)
    forced = jax.random.randint(key_force, (), 0, half).astype(jnp.int32)
    side = jax.random.randint(key_side, (), 0, 2).astype(jnp.int32)
    positions = jnp.arange(half, dtype=jnp.int32)
    kinds = jnp.where(positions == forced, 3 + side, kinds)
    lower = first_table[kinds]
    upper = second_table[kinds]
    return jnp.concatenate([lower, upper]).astype(jnp.int32)


def with_spikes(values, rng, source, target, shards_of, factor):
    def block_of(axis_at):
        return (jnp.arange(values.shape[axis_at]) // (values.shape[axis_at] // shards_of)).reshape((-1,) + (1,) * (values.ndim - 1 - axis_at))

    first = jax.random.permutation(rng, shards_of)[block_of(target)]
    far = (block_of(target) + shards_of // 2) % shards_of
    return jnp.where((block_of(source) == first) | (block_of(source) == far), factor * values, values)


def level_of(own_key, dims, shards, least, high):
    factor_of = 1.0
    for dim, shards_of in shards:
        heights = jax.random.uniform(jax.random.fold_in(jax.random.fold_in(own_key, 6), dim), (shards_of,), jnp.float32, least / len(shards), high / len(shards))
        factor_of = factor_of * jnp.repeat(jnp.exp(heights), dims[dim] // shards_of).reshape((-1,) + (1,) * (len(dims) - 1 - dim))
    return factor_of


def bell_draw(key, dims, scale, most, cuts=(), kind=jnp.bfloat16):
    loudness = level_of(key, dims, cuts, -0.22, 0.18) if cuts else 1.0
    values = jax.random.normal(key, dims, jnp.float32) * scale * loudness
    return jnp.minimum(jnp.maximum(values, -most), most).astype(kind)


def heavy_noise(key, extent, deviation, most, cuts, heavy, kind=jnp.bfloat16):
    drawn = deviation * jax.random.normal(key, extent, jnp.float32)
    if cuts:
        drawn = drawn * level_of(key, extent, cuts, -0.22, 0.18)
    return jnp.clip(with_spikes(drawn, jax.random.fold_in(key, 3), *heavy), -most, most).astype(kind)


def setup_inputs(seed: int = 0, part: int = 0) -> dict:
    key_list = jax.random.split(jax.random.key(seed), 6)
    own_keys = jax.random.split(jax.random.fold_in(key_list[5], part), 6)
    upstream = heavy_noise(own_keys[0], (ROWS, D), 1.0, 6.0, ((0, 4),), (0, 1, 4, 2.0))
    attn = bell_draw(own_keys[1], (ROWS, D), 1.0, 6.0, ((0, 4), (1, 4)))
    gate = bell_draw(own_keys[2], (N_DP, D), 1.0, 4.0, ((0, 4),))
    visible = draw_visible(jax.random.fold_in(jax.random.fold_in(key_list[5], part), 71), part)
    proj_weight = bell_draw(key_list[4], (D, D), D ** -0.5, 0.09375, ((0, 4), (1, 4)))
    return dict(upstream=upstream, attn=attn, gate=gate, visible=visible, proj_weight=proj_weight)


def reference(upstream, attn, gate, visible, proj_weight):
    row_index = jnp.arange(ROWS, dtype=jnp.int32)
    slot = row_index % CAP
    limit = jnp.repeat(visible, CAP, axis=0) * BLOCK
    live = (slot < limit)[:, None]
    gate_rows = jnp.repeat(gate, CAP, axis=0).astype(jnp.float32)
    grad_proj = jnp.where(live, gate_rows * upstream.astype(jnp.float32), 0.0).astype(jnp.bfloat16)
    grad_attn = jnp.dot(grad_proj, proj_weight.T, preferred_element_type=jnp.float32).astype(jnp.bfloat16)
    scale = 1.0 / jnp.sqrt(jnp.float32(ROWS))
    grad_weight = (jnp.dot(attn.T, grad_proj, preferred_element_type=jnp.float32) * scale).astype(jnp.bfloat16)
    return (grad_attn, grad_weight)
```

```python
import functools

import jax
import jax.numpy as jnp
import numpy as np
from jax import lax
from jax.experimental import pallas as pl
from jax.experimental.pallas import tpu as pltpu
from jax.sharding import PartitionSpec as P

BLOCK = 128
BLOCKS = 4
LIVE = 3
PIECES = 4
MESH = pl.DeviceIdType.MESH
F32 = jnp.float32
BF16 = jnp.bfloat16


def kernel(
    n, scale,
    up_ref, attn_ref, gate_ref, visible_ref, w_ref,
    ga_ref, gw_ref,
    uq, uc, attn, w, gq, gp, part, total, up_in, up_out, dn_in, dn_out,
    load_sem, gp_send, gp_recv, sh_send, sh_recv, up_send, up_recv, dn_send, dn_recv,
):
    half = n // 2
    heads, cols = w_ref.shape
    tile = min(256, heads)
    d = lax.axis_index("dp")
    mp = lax.axis_index("mp")
    sub = lax.axis_index("sub")
    mbit = mp % 2
    q = 2 * mbit + sub
    low = (d < half).astype(jnp.int32)
    visible = visible_ref[0]

    def base(image):
        return (image >= half).astype(jnp.int32)

    def block_of(slot):
        return low * slot + (1 - low) * (BLOCKS - 1 - slot)

    def live(slot):
        return (block_of(slot) < visible).astype(F32)

    def peer(r):
        other_m = mp + (r // 2) * (1 - 2 * mbit)
        other_s = sub + (r % 2) * (1 - 2 * sub)
        return {"mp": other_m, "sub": other_s}

    def piece_of(r):
        return 2 * (mbit + (r // 2) * (1 - 2 * mbit)) + sub + (r % 2) * (1 - 2 * sub)

    my_base = base(d)
    loads = []
    for t in range(LIVE):
        b = block_of(my_base + t)
        loads.append(pltpu.make_async_copy(up_ref.at[b, q], uq.at[t], load_sem.at[t]))
    own_cols = pl.ds(pl.multiple_of(d * cols, cols), cols)
    for t in range(LIVE):
        b = block_of(my_base + t)
        loads.append(pltpu.make_async_copy(up_ref.at[b, :, :, own_cols], uc.at[t], load_sem.at[LIVE + t]))
    loads.append(pltpu.make_async_copy(w_ref, w, load_sem.at[2 * LIVE]))
    for s in range(BLOCKS):
        loads.append(pltpu.make_async_copy(attn_ref.at[block_of(s)], attn.at[s], load_sem.at[2 * LIVE + 1 + s]))
    for load in loads:
        load.start()

    barrier = pltpu.get_barrier_semaphore()
    for k in range(1, n):
        pl.semaphore_signal(barrier, inc=1, device_id={"dp": lax.rem(d + k, n)}, device_id_type=MESH)
    for r in range(1, PIECES):
        pl.semaphore_signal(barrier, inc=1, device_id=peer(r), device_id_type=MESH)
    pl.semaphore_wait(barrier, n - 1 + PIECES - 1)

    def gp_copy(target, source):
        return pltpu.make_async_remote_copy(
            src_ref=gq.at[target], dst_ref=gp.at[source, :, q],
            send_sem=gp_send.at[target], recv_sem=gp_recv.at[source],
            device_id={"dp": target}, device_id_type=MESH,
        )

    def share_copy(image, r, piece):
        return pltpu.make_async_remote_copy(
            src_ref=gp.at[image, :, piece], dst_ref=gp.at[image, :, piece],
            send_sem=sh_send.at[image, r - 1], recv_sem=sh_recv.at[image, r - 1],
            device_id=peer(r), device_id_type=MESH,
        )

    for load in loads[:LIVE]:
        load.wait()

    @pl.loop(1, n)
    def _(k):
        target = lax.rem(d + k, n)
        at = pl.ds(pl.multiple_of(target * cols, cols), cols)
        gate = gate_ref[:, at].astype(F32)
        for t in range(LIVE):
            value = uq[t, :, at].astype(F32) * gate * live(my_base + t)
            gq[target, t] = value.astype(BF16)
        gp_copy(target, d).start()

    for load in loads[LIVE:2 * LIVE]:
        load.wait()
    own_gate = gate_ref[:, own_cols].astype(F32)
    for t in range(LIVE):
        value = uc[t].astype(F32) * own_gate.reshape(1, 1, cols) * live(my_base + t)
        gp[d, t] = value.astype(BF16)
    for load in loads[2 * LIVE:]:
        load.wait()

    def rows_of(image):
        return gp[image].reshape(LIVE * BLOCK, cols)

    def project(image):
        @pl.loop(0, heads // tile)
        def _(j):
            at = pl.ds(pl.multiple_of(j * tile, tile), tile)
            out = lax.dot_general(rows_of(image), w[at, :], (((1,), (1,)), ((), ())), preferred_element_type=F32)
            part[image, pl.ds(base(image), LIVE), :, at] = out.reshape(LIVE, BLOCK, tile)
        part[image, (1 - base(image)) * (BLOCKS - 1)] = jnp.zeros((BLOCK, heads), F32)

    def accumulate(image, read):
        @pl.loop(0, heads // tile)
        def _(j):
            at = pl.ds(pl.multiple_of(j * tile, tile), tile)
            left = read(base(image), at).reshape(LIVE * BLOCK, tile)
            total[at, :] += lax.dot_general(
                left, rows_of(image), (((0,), (0,)), ((), ())), preferred_element_type=F32
            )

    @pl.loop(0, n)
    def _(k):
        @pl.when(k >= 1)
        def _():
            image = lax.rem(d + n - k, n)
            gp_copy(lax.rem(d + k, n), image).wait_recv()
            for r in range(1, PIECES):
                share_copy(image, r, q).start()

        @pl.when(k >= 2)
        def _():
            image = lax.rem(d + n - k + 1, n)
            for r in range(1, PIECES):
                share_copy(image, r, piece_of(r)).wait_recv()
            project(image)

        @pl.when(k == 0)
        def _():
            project(d)

    last = lax.rem(d + 1, n)
    for r in range(1, PIECES):
        share_copy(last, r, piece_of(r)).wait_recv()
    project(last)

    total[...] = jnp.zeros_like(total)
    accumulate(d, lambda first, at: attn[pl.ds(first, LIVE), :, at])

    def chain_copy(step, out, into, send, recv, target):
        return pltpu.make_async_remote_copy(
            src_ref=out.at[step], dst_ref=into.at[step], send_sem=send.at[step], recv_sem=recv.at[step],
            device_id={"dp": target}, device_id_type=MESH,
        )

    steps = half * BLOCKS

    def advance(step, position, shift, into, out, send, recv):
        lane, slot = step // BLOCKS, step % BLOCKS
        target = lax.rem(d + n + shift, n)

        @pl.when(position == 0)
        def _():
            into[step] = jnp.zeros((BLOCK, heads), BF16)

        @pl.when(position > 0)
        def _():
            chain_copy(step, out, into, send, recv, target).wait_recv()

        @pl.when(position < n - 1)
        def _():
            ahead_lo = (shift * (lane - d) > 0).astype(F32)
            ahead_hi = (shift * (lane + half - d) > 0).astype(F32)
            keep = (lax.rem(d, half) == lane).astype(F32) * live(slot)
            value = keep * attn[slot].astype(F32) + (1.0 - keep) * into[step].astype(F32)
            value += ahead_lo * part[lane, slot] + ahead_hi * part[lane + half, slot]
            out[step] = value.astype(BF16)
            chain_copy(step, out, into, send, recv, target).start()

        @pl.when(slot == BLOCKS - 1)
        def _():
            for image in (lane, lane + half):
                @pl.when(shift * (image - d) < 0)
                def _():
                    accumulate(
                        image,
                        lambda first, at: into[pl.ds(lane * BLOCKS + first, LIVE), :, at],
                    )

    @pl.loop(0, steps + n - 1)
    def _(time):
        up, down = time - d, time - (n - 1 - d)

        @pl.when((up >= 0) & (up < steps))
        def _():
            advance(up, d, 1, up_in, up_out, up_send, up_recv)

        @pl.when((down >= 0) & (down < steps))
        def _():
            advance(down, n - 1 - d, -1, dn_in, dn_out, dn_send, dn_recv)

    lane = lax.rem(d, half)
    for t in range(LIVE):
        slot = my_base + t
        at = lane * BLOCKS + slot
        value = up_in[at].astype(F32) + dn_in[at].astype(F32) + part[d, slot]
        ga_ref[block_of(slot)] = (value * live(slot)).astype(BF16)
    ga_ref[BLOCKS - 1] = jnp.zeros((BLOCK, heads), BF16)

    @pl.loop(0, heads // tile)
    def _(j):
        at = pl.ds(pl.multiple_of(j * tile, tile), tile)
        gw_ref[at, :] = (total[at, :] * scale).astype(BF16)

    @pl.loop(1, n)
    def _(k):
        gp_copy(lax.rem(d + k, n), d).wait_send()
        for r in range(1, PIECES):
            share_copy(lax.rem(d + k, n), r, q).wait_send()

    @pl.loop(0, steps)
    def _(step):
        @pl.when(d < n - 1)
        def _():
            chain_copy(step, up_out, up_in, up_send, up_recv, lax.rem(d + 1, n)).wait_send()

        @pl.when(d > 0)
        def _():
            chain_copy(step, dn_out, dn_in, dn_send, dn_recv, lax.rem(d + n - 1, n)).wait_send()


def per_device(upstream, attn, gate, visible, proj_weight):
    slots, width = upstream.shape
    heads, cols = proj_weight.shape
    n = lax.axis_size("dp")
    rows = BLOCK // PIECES
    steps = n // 2 * BLOCKS
    scale = float(1.0 / np.sqrt(np.float32(slots * n)))
    any_space = pl.BlockSpec(memory_space=pl.ANY)
    in_vmem = pl.BlockSpec(memory_space=pltpu.VMEM)
    dma = pltpu.SemaphoreType.DMA
    grad_attn, grad_weight = pl.pallas_call(
        functools.partial(kernel, n, scale),
        out_shape=(
            jax.ShapeDtypeStruct((BLOCKS, BLOCK, heads), BF16),
            jax.ShapeDtypeStruct((heads, cols), BF16),
        ),
        in_specs=[any_space, any_space, in_vmem, pl.BlockSpec(memory_space=pltpu.SMEM), any_space],
        out_specs=(in_vmem, in_vmem),
        scratch_shapes=[
            pltpu.VMEM((LIVE, rows, width), BF16),
            pltpu.VMEM((LIVE, PIECES, rows, cols), BF16),
            pltpu.VMEM((BLOCKS, BLOCK, heads), BF16),
            pltpu.VMEM((heads, cols), BF16),
            pltpu.VMEM((n, LIVE, rows, cols), BF16),
            pltpu.VMEM((n, LIVE, PIECES, rows, cols), BF16),
            pltpu.VMEM((n, BLOCKS, BLOCK, heads), F32),
            pltpu.VMEM((heads, cols), F32),
            pltpu.VMEM((steps, BLOCK, heads), BF16),
            pltpu.VMEM((steps, BLOCK, heads), BF16),
            pltpu.VMEM((steps, BLOCK, heads), BF16),
            pltpu.VMEM((steps, BLOCK, heads), BF16),
            dma((2 * LIVE + 1 + BLOCKS,)),
            dma((n,)), dma((n,)),
            dma((n, PIECES - 1)), dma((n, PIECES - 1)),
            dma((steps,)), dma((steps,)), dma((steps,)), dma((steps,)),
        ],
        compiler_params=pltpu.CompilerParams(
            collective_id=0, has_side_effects=True, vmem_limit_bytes=56 * 1024 * 1024
        ),
    )(
        upstream.reshape(BLOCKS, PIECES, rows, width),
        attn.reshape(BLOCKS, BLOCK, heads),
        gate,
        visible,
        proj_weight,
    )
    return grad_attn.reshape(slots, heads), grad_weight


def solution(mesh):
    return jax.shard_map(
        per_device,
        mesh=mesh,
        in_specs=(
            P(("groups", "dp"), None),
            P(("groups", "dp"), ("mp", "sub")),
            P(("groups", "dp"), None),
            P(("groups", "dp")),
            P(("mp", "sub"), "dp"),
        ),
        out_specs=(P(("groups", "dp"), ("mp", "sub")), P(("mp", "sub"), ("groups", "dp"))),
        check_vma=False,
    )
```

```python
import functools

import jax
import jax.numpy as jnp
import numpy as np
from jax import lax
from jax.experimental import pallas as pl
from jax.experimental.pallas import tpu as pltpu
from jax.sharding import PartitionSpec as P

BLOCK = 128
BLOCKS = 4
LIVE = 3
SPLIT = 1
PIECES = 4
MESH = pl.DeviceIdType.MESH
F32 = jnp.float32
BF16 = jnp.bfloat16


def kernel(
    n, scale,
    up_ref, attn_ref, gate_ref, visible_ref, w_ref,
    ga_ref, gw_ref,
    uq, uc, attn, w, gq, gp, part, total, up_in, up_out, dn_in, dn_out,
    load_sem, gp_send, gp_recv, sh_send, sh_recv, up_send, up_recv, dn_send, dn_recv,
):
    half = n // 2
    heads, cols = w_ref.shape
    tile = min(256, heads)
    thin = BLOCK // SPLIT
    d = lax.axis_index("dp")
    mp = lax.axis_index("mp")
    sub = lax.axis_index("sub")
    mbit = mp % 2
    q = 2 * mbit + sub
    low = (d < half).astype(jnp.int32)
    visible = visible_ref[0]

    def base(image):
        return (image >= half).astype(jnp.int32)

    def block_of(slot):
        return low * slot + (1 - low) * (BLOCKS - 1 - slot)

    def live(slot):
        return (block_of(slot) < visible).astype(F32)

    def peer(r):
        other_m = mp + (r // 2) * (1 - 2 * mbit)
        other_s = sub + (r % 2) * (1 - 2 * sub)
        return {"mp": other_m, "sub": other_s}

    def piece_of(r):
        return 2 * (mbit + (r // 2) * (1 - 2 * mbit)) + sub + (r % 2) * (1 - 2 * sub)

    my_base = base(d)
    loads = []
    for t in range(LIVE):
        b = block_of(my_base + t)
        loads.append(pltpu.make_async_copy(up_ref.at[b, q], uq.at[t], load_sem.at[t]))
    own_cols = pl.ds(pl.multiple_of(d * cols, cols), cols)
    for t in range(LIVE):
        b = block_of(my_base + t)
        loads.append(pltpu.make_async_copy(up_ref.at[b, :, :, own_cols], uc.at[t], load_sem.at[LIVE + t]))
    loads.append(pltpu.make_async_copy(w_ref, w, load_sem.at[2 * LIVE]))
    for s in range(BLOCKS):
        loads.append(pltpu.make_async_copy(attn_ref.at[block_of(s)], attn.at[s], load_sem.at[2 * LIVE + 1 + s]))
    for load in loads:
        load.start()

    barrier = pltpu.get_barrier_semaphore()
    for k in range(1, n):
        pl.semaphore_signal(barrier, inc=1, device_id={"dp": lax.rem(d + k, n)}, device_id_type=MESH)
    for r in range(1, PIECES):
        pl.semaphore_signal(barrier, inc=1, device_id=peer(r), device_id_type=MESH)
    pl.semaphore_wait(barrier, n - 1 + PIECES - 1)

    def gp_copy(target, source):
        return pltpu.make_async_remote_copy(
            src_ref=gq.at[target], dst_ref=gp.at[source, :, q],
            send_sem=gp_send.at[target], recv_sem=gp_recv.at[source],
            device_id={"dp": target}, device_id_type=MESH,
        )

    def share_copy(image, r, piece):
        return pltpu.make_async_remote_copy(
            src_ref=gp.at[image, :, piece], dst_ref=gp.at[image, :, piece],
            send_sem=sh_send.at[image, r - 1], recv_sem=sh_recv.at[image, r - 1],
            device_id=peer(2 if r == 2 else 1), device_id_type=MESH,
        )

    def finish_share(image):
        share_copy(image, 2, piece_of(2)).wait_recv()
        share_copy(image, 3, piece_of(2)).start()
        share_copy(image, 1, piece_of(1)).wait_recv()
        share_copy(image, 3, piece_of(3)).wait_recv()

    for load in loads[:LIVE]:
        load.wait()

    @pl.loop(1, n)
    def _(k):
        target = lax.rem(d + k, n)
        at = pl.ds(pl.multiple_of(target * cols, cols), cols)
        gate = gate_ref[:, at].astype(F32)
        for t in range(LIVE):
            value = uq[t, :, at].astype(F32) * gate * live(my_base + t)
            gq[target, t] = value.astype(BF16)
        gp_copy(target, d).start()

    for load in loads[LIVE:2 * LIVE]:
        load.wait()
    own_gate = gate_ref[:, own_cols].astype(F32)
    for t in range(LIVE):
        value = uc[t].astype(F32) * own_gate.reshape(1, 1, cols) * live(my_base + t)
        gp[d, t] = value.astype(BF16)
    for load in loads[2 * LIVE:]:
        load.wait()

    def rows_of(image):
        return gp[image].reshape(LIVE * BLOCK, cols)

    def project(image):
        @pl.loop(0, heads // tile)
        def _(j):
            at = pl.ds(pl.multiple_of(j * tile, tile), tile)
            out = lax.dot_general(rows_of(image), w[at, :], (((1,), (1,)), ((), ())), preferred_element_type=F32)
            part[image, pl.ds(base(image), LIVE), :, :, at] = out.reshape(LIVE, SPLIT, thin, tile)
        part[image, (1 - base(image)) * (BLOCKS - 1)] = jnp.zeros((SPLIT, thin, heads), F32)

    def accumulate(image, read):
        @pl.loop(0, heads // tile)
        def _(j):
            at = pl.ds(pl.multiple_of(j * tile, tile), tile)
            left = read(base(image), at).reshape(LIVE * BLOCK, tile)
            total[at, :] += lax.dot_general(
                left, rows_of(image), (((0,), (0,)), ((), ())), preferred_element_type=F32
            )

    steps = half * BLOCKS * SPLIT
    pure = (1 - low) * (BLOCKS - 1)

    def chain_copy(step, source, into, send, recv, target):
        return pltpu.make_async_remote_copy(
            src_ref=source, dst_ref=into.at[step], send_sem=send.at[step], recv_sem=recv.at[step],
            device_id={"dp": target}, device_id_type=MESH,
        )

    def send_pure(position, shift, into, send, recv):
        @pl.when(position < n - 1)
        def _():
            for p in range(SPLIT):
                step = (lax.rem(d, half) * BLOCKS + pure) * SPLIT + p
                chain_copy(step, attn.at[pure, p], into, send, recv, lax.rem(d + n + shift, n)).start()

    @pl.loop(0, n)
    def _(k):
        @pl.when(k == n - 1)
        def _():
            image = lax.rem(d + n - k, n)
            gp_copy(lax.rem(d + k, n), image).wait_recv()
            share_copy(image, 2, q).start()
            share_copy(image, 1, q).start()
            send_pure(d, 1, up_in, up_send, up_recv)
            send_pure(n - 1 - d, -1, dn_in, dn_send, dn_recv)

        @pl.when((k >= 1) & (k < n - 1))
        def _():
            image = lax.rem(d + n - k, n)
            gp_copy(lax.rem(d + k, n), image).wait_recv()
            share_copy(image, 2, q).start()
            share_copy(image, 1, q).start()

        @pl.when(k >= 2)
        def _():
            image = lax.rem(d + n - k + 1, n)
            finish_share(image)
            project(image)

        @pl.when(k == 0)
        def _():
            project(d)

    last = lax.rem(d + 1, n)
    finish_share(last)
    project(last)

    total[...] = jnp.zeros_like(total)
    accumulate(d, lambda first, at: attn[pl.ds(first, LIVE), :, :, at])

    def advance(step, position, shift, into, out, send, recv):
        lane, slot, p = step // (BLOCKS * SPLIT), step // SPLIT % BLOCKS, step % SPLIT
        target = lax.rem(d + n + shift, n)

        @pl.when(position == 0)
        def _():
            into[step] = jnp.zeros((thin, heads), BF16)

        @pl.when(position > 0)
        def _():
            chain_copy(step, out.at[step], into, send, recv, target).wait_recv()

        @pl.when((position < n - 1) & ((lane != lax.rem(d, half)) | (slot != pure)))
        def _():
            ahead_lo = (shift * (lane - d) > 0).astype(F32)
            ahead_hi = (shift * (lane + half - d) > 0).astype(F32)
            keep = (lax.rem(d, half) == lane).astype(F32) * live(slot)
            value = keep * attn[slot, p].astype(F32) + (1.0 - keep) * into[step].astype(F32)
            value += ahead_lo * part[lane, slot, p] + ahead_hi * part[lane + half, slot, p]
            out[step] = value.astype(BF16)
            chain_copy(step, out.at[step], into, send, recv, target).start()

        @pl.when(step % (BLOCKS * SPLIT) == BLOCKS * SPLIT - 1)
        def _():
            for image in (lane, lane + half):
                @pl.when(shift * (image - d) < 0)
                def _():
                    accumulate(
                        image,
                        lambda first, at: into[pl.ds((lane * BLOCKS + first) * SPLIT, LIVE * SPLIT), :, at],
                    )

    @pl.loop(0, max(2 * steps, steps + n - 1))
    def _(time):
        up = time - jnp.where(d == n - 1, steps, d)
        down = time - jnp.where(d == 0, steps, n - 1 - d)

        @pl.when((up >= 0) & (up < steps))
        def _():
            advance(up, d, 1, up_in, up_out, up_send, up_recv)

        @pl.when((down >= 0) & (down < steps))
        def _():
            advance(down, n - 1 - d, -1, dn_in, dn_out, dn_send, dn_recv)

    lane = lax.rem(d, half)
    for t in range(LIVE):
        slot = my_base + t
        at = pl.ds((lane * BLOCKS + slot) * SPLIT, SPLIT)
        value = up_in[at].astype(F32) + dn_in[at].astype(F32) + part[d, slot]
        ga_ref[block_of(slot)] = (value * live(slot)).astype(BF16)
    ga_ref[BLOCKS - 1] = jnp.zeros((SPLIT, thin, heads), BF16)

    @pl.loop(0, heads // tile)
    def _(j):
        at = pl.ds(pl.multiple_of(j * tile, tile), tile)
        gw_ref[at, :] = (total[at, :] * scale).astype(BF16)

    @pl.loop(1, n)
    def _(k):
        gp_copy(lax.rem(d + k, n), d).wait_send()
        for r in range(1, PIECES):
            share_copy(lax.rem(d + k, n), r, piece_of(2) if r == 3 else q).wait_send()

    @pl.loop(0, steps)
    def _(step):
        @pl.when(d < n - 1)
        def _():
            chain_copy(step, up_out.at[step], up_in, up_send, up_recv, lax.rem(d + 1, n)).wait_send()

        @pl.when(d > 0)
        def _():
            chain_copy(step, dn_out.at[step], dn_in, dn_send, dn_recv, lax.rem(d + n - 1, n)).wait_send()


def per_device(upstream, attn, gate, visible, proj_weight):
    slots, width = upstream.shape
    heads, cols = proj_weight.shape
    n = lax.axis_size("dp")
    rows = BLOCK // PIECES
    steps = n // 2 * BLOCKS * SPLIT
    thin = BLOCK // SPLIT
    scale = float(1.0 / np.sqrt(np.float32(slots * n)))
    any_space = pl.BlockSpec(memory_space=pl.ANY)
    in_vmem = pl.BlockSpec(memory_space=pltpu.VMEM)
    dma = pltpu.SemaphoreType.DMA
    grad_attn, grad_weight = pl.pallas_call(
        functools.partial(kernel, n, scale),
        out_shape=(
            jax.ShapeDtypeStruct((BLOCKS, SPLIT, thin, heads), BF16),
            jax.ShapeDtypeStruct((heads, cols), BF16),
        ),
        in_specs=[any_space, any_space, in_vmem, pl.BlockSpec(memory_space=pltpu.SMEM), any_space],
        out_specs=(in_vmem, in_vmem),
        scratch_shapes=[
            pltpu.VMEM((LIVE, rows, width), BF16),
            pltpu.VMEM((LIVE, PIECES, rows, cols), BF16),
            pltpu.VMEM((BLOCKS, SPLIT, thin, heads), BF16),
            pltpu.VMEM((heads, cols), BF16),
            pltpu.VMEM((n, LIVE, rows, cols), BF16),
            pltpu.VMEM((n, LIVE, PIECES, rows, cols), BF16),
            pltpu.VMEM((n, BLOCKS, SPLIT, thin, heads), F32),
            pltpu.VMEM((heads, cols), F32),
            pltpu.VMEM((steps, thin, heads), BF16),
            pltpu.VMEM((steps, thin, heads), BF16),
            pltpu.VMEM((steps, thin, heads), BF16),
            pltpu.VMEM((steps, thin, heads), BF16),
            dma((2 * LIVE + 1 + BLOCKS,)),
            dma((n,)), dma((n,)),
            dma((n, PIECES - 1)), dma((n, PIECES - 1)),
            dma((steps,)), dma((steps,)), dma((steps,)), dma((steps,)),
        ],
        compiler_params=pltpu.CompilerParams(
            collective_id=0, has_side_effects=True, vmem_limit_bytes=56 * 1024 * 1024
        ),
    )(
        upstream.reshape(BLOCKS, PIECES, rows, width),
        attn.reshape(BLOCKS, SPLIT, thin, heads),
        gate,
        visible,
        proj_weight,
    )
    return grad_attn.reshape(slots, heads), grad_weight


def solution(mesh):
    return jax.shard_map(
        per_device,
        mesh=mesh,
        in_specs=(
            P(("groups", "dp"), None),
            P(("groups", "dp"), ("mp", "sub")),
            P(("groups", "dp"), None),
            P(("groups", "dp")),
            P(("mp", "sub"), "dp"),
        ),
        out_specs=(P(("groups", "dp"), ("mp", "sub")), P(("mp", "sub"), ("groups", "dp"))),
        check_vma=False,
    )
```

```python
import functools

import jax
import jax.numpy as jnp
import numpy as np
from jax import lax
from jax.experimental import pallas as pl
from jax.experimental.pallas import tpu as pltpu
from jax.sharding import PartitionSpec as P

BLOCK = 128
BLOCKS = 4
LIVE = 3
SPLIT = 1
PIECES = 4
MESH = pl.DeviceIdType.MESH
F32 = jnp.float32
BF16 = jnp.bfloat16


def kernel(
    n, scale,
    up_ref, attn_ref, gate_ref, visible_ref, w_ref,
    ga_ref, gw_ref,
    uq, uc, attn, w, gq, gp, part, total, up_in, up_out, dn_in, dn_out,
    load_sem, gp_send, gp_recv, sh_send, sh_recv, up_send, up_recv, dn_send, dn_recv,
):
    half = n // 2
    heads, cols = w_ref.shape
    tile = min(256, heads)
    thin = BLOCK // SPLIT
    d = lax.axis_index("dp")
    mp = lax.axis_index("mp")
    sub = lax.axis_index("sub")
    mbit = mp % 2
    q = 2 * mbit + sub
    low = (d < half).astype(jnp.int32)
    visible = visible_ref[0]

    def base(image):
        return (image >= half).astype(jnp.int32)

    def block_of(slot):
        return low * slot + (1 - low) * (BLOCKS - 1 - slot)

    def live(slot):
        return (block_of(slot) < visible).astype(F32)

    def peer(r):
        other_m = mp + (r // 2) * (1 - 2 * mbit)
        other_s = sub + (r % 2) * (1 - 2 * sub)
        return {"mp": other_m, "sub": other_s}

    def piece_of(r):
        return 2 * (mbit + (r // 2) * (1 - 2 * mbit)) + sub + (r % 2) * (1 - 2 * sub)

    my_base = base(d)
    loads = []
    for t in range(LIVE):
        b = block_of(my_base + t)
        loads.append(pltpu.make_async_copy(up_ref.at[b, q], uq.at[t], load_sem.at[t]))
    own_cols = pl.ds(pl.multiple_of(d * cols, cols), cols)
    for t in range(LIVE):
        b = block_of(my_base + t)
        loads.append(pltpu.make_async_copy(up_ref.at[b, :, :, own_cols], uc.at[t], load_sem.at[LIVE + t]))
    loads.append(pltpu.make_async_copy(w_ref, w, load_sem.at[2 * LIVE]))
    for s in range(BLOCKS):
        loads.append(pltpu.make_async_copy(attn_ref.at[block_of(s)], attn.at[s], load_sem.at[2 * LIVE + 1 + s]))
    for load in loads:
        load.start()

    barrier = pltpu.get_barrier_semaphore()
    for k in range(1, n):
        pl.semaphore_signal(barrier, inc=1, device_id={"dp": lax.rem(d + k, n)}, device_id_type=MESH)
    for r in range(1, PIECES):
        pl.semaphore_signal(barrier, inc=1, device_id=peer(r), device_id_type=MESH)
    pl.semaphore_wait(barrier, n - 1 + PIECES - 1)

    def gp_copy(target, source):
        return pltpu.make_async_remote_copy(
            src_ref=gq.at[target], dst_ref=gp.at[source, :, q],
            send_sem=gp_send.at[target], recv_sem=gp_recv.at[source],
            device_id={"dp": target}, device_id_type=MESH,
        )

    def share_copy(image, r, piece):
        return pltpu.make_async_remote_copy(
            src_ref=gp.at[image, :, piece], dst_ref=gp.at[image, :, piece],
            send_sem=sh_send.at[image, r - 1], recv_sem=sh_recv.at[image, r - 1],
            device_id=peer(2 if r == 2 else 1), device_id_type=MESH,
        )

    def finish_share(image):
        share_copy(image, 2, piece_of(2)).wait_recv()
        share_copy(image, 3, piece_of(2)).start()
        share_copy(image, 1, piece_of(1)).wait_recv()
        share_copy(image, 3, piece_of(3)).wait_recv()

    for load in loads[:LIVE]:
        load.wait()

    @pl.loop(1, n)
    def _(k):
        target = lax.rem(d + k, n)
        at = pl.ds(pl.multiple_of(target * cols, cols), cols)
        gate = gate_ref[:, at].astype(F32)
        for t in range(LIVE):
            value = uq[t, :, at].astype(F32) * gate * live(my_base + t)
            gq[target, t] = value.astype(BF16)
        gp_copy(target, d).start()

    for load in loads[LIVE:2 * LIVE]:
        load.wait()
    own_gate = gate_ref[:, own_cols].astype(F32)
    for t in range(LIVE):
        value = uc[t].astype(F32) * own_gate.reshape(1, 1, cols) * live(my_base + t)
        gp[d, t] = value.astype(BF16)
    for load in loads[2 * LIVE:]:
        load.wait()

    def rows_of(image):
        return gp[image].reshape(LIVE * BLOCK, cols)

    def project(image):
        @pl.loop(0, heads // tile)
        def _(j):
            at = pl.ds(pl.multiple_of(j * tile, tile), tile)
            out = lax.dot_general(rows_of(image), w[at, :], (((1,), (1,)), ((), ())), preferred_element_type=F32)
            part[image, pl.ds(base(image), LIVE), :, :, at] = out.reshape(LIVE, SPLIT, thin, tile)
        part[image, (1 - base(image)) * (BLOCKS - 1)] = jnp.zeros((SPLIT, thin, heads), F32)

    def accumulate(image, read):
        @pl.loop(0, heads // tile)
        def _(j):
            at = pl.ds(pl.multiple_of(j * tile, tile), tile)
            left = read(base(image), at).reshape(LIVE * BLOCK, tile)
            total[at, :] += lax.dot_general(
                left, rows_of(image), (((0,), (0,)), ((), ())), preferred_element_type=F32
            )

    steps = half * BLOCKS * SPLIT
    pure = (1 - low) * (BLOCKS - 1)

    def chain_copy(step, source, into, send, recv, target):
        return pltpu.make_async_remote_copy(
            src_ref=source, dst_ref=into.at[step], send_sem=send.at[step], recv_sem=recv.at[step],
            device_id={"dp": target}, device_id_type=MESH,
        )

    def send_pure(position, shift, into, send, recv):
        @pl.when(position < n - 1)
        def _():
            for p in range(SPLIT):
                step = (lax.rem(d, half) * BLOCKS + pure) * SPLIT + p
                chain_copy(step, attn.at[pure, p], into, send, recv, lax.rem(d + n + shift, n)).start()

    @pl.loop(0, n)
    def _(k):
        @pl.when(k == n - 1)
        def _():
            image = lax.rem(d + n - k, n)
            gp_copy(lax.rem(d + k, n), image).wait_recv()
            share_copy(image, 2, q).start()
            share_copy(image, 1, q).start()
            send_pure(d, 1, up_in, up_send, up_recv)
            send_pure(n - 1 - d, -1, dn_in, dn_send, dn_recv)

        @pl.when((k >= 1) & (k < n - 1))
        def _():
            image = lax.rem(d + n - k, n)
            gp_copy(lax.rem(d + k, n), image).wait_recv()
            share_copy(image, 2, q).start()
            share_copy(image, 1, q).start()

        @pl.when(k >= 2)
        def _():
            image = lax.rem(d + n - k + 1, n)
            finish_share(image)
            project(image)

        @pl.when(k == 0)
        def _():
            project(d)

        @pl.when(k == 1)
        def _():
            total[...] = jnp.zeros_like(total)
            accumulate(d, lambda first, at: attn[pl.ds(first, LIVE), :, :, at])

    last = lax.rem(d + 1, n)
    finish_share(last)
    project(last)


    def advance(step, position, shift, into, out, send, recv):
        lane, slot, p = step // (BLOCKS * SPLIT), step // SPLIT % BLOCKS, step % SPLIT
        target = lax.rem(d + n + shift, n)

        @pl.when(position == 0)
        def _():
            into[step] = jnp.zeros((thin, heads), BF16)

        @pl.when(position > 0)
        def _():
            chain_copy(step, out.at[step], into, send, recv, target).wait_recv()

        @pl.when((position < n - 1) & ((lane != lax.rem(d, half)) | (slot != pure)))
        def _():
            ahead_lo = (shift * (lane - d) > 0).astype(F32)
            ahead_hi = (shift * (lane + half - d) > 0).astype(F32)
            keep = (lax.rem(d, half) == lane).astype(F32) * live(slot)
            value = keep * attn[slot, p].astype(F32) + (1.0 - keep) * into[step].astype(F32)
            value += ahead_lo * part[lane, slot, p] + ahead_hi * part[lane + half, slot, p]
            out[step] = value.astype(BF16)
            chain_copy(step, out.at[step], into, send, recv, target).start()

        image = lane + half * (slot - LIVE + 1)

        @pl.when((slot >= LIVE - 1) & (p == SPLIT - 1) & (shift * (image - d) < 0))
        def _():
            accumulate(
                image,
                lambda first, at: into[pl.ds((lane * BLOCKS + first) * SPLIT, LIVE * SPLIT), :, at],
            )

    @pl.loop(0, max(2 * steps, steps + n - 1))
    def _(time):
        up = time - jnp.where(d == n - 1, steps, d)
        down = time - jnp.where(d == 0, steps, n - 1 - d)

        @pl.when((up >= 0) & (up < steps))
        def _():
            advance(up, d, 1, up_in, up_out, up_send, up_recv)

        @pl.when((down >= 0) & (down < steps))
        def _():
            advance(down, n - 1 - d, -1, dn_in, dn_out, dn_send, dn_recv)

    lane = lax.rem(d, half)
    for t in range(LIVE):
        slot = my_base + t
        at = pl.ds((lane * BLOCKS + slot) * SPLIT, SPLIT)
        value = up_in[at].astype(F32) + dn_in[at].astype(F32) + part[d, slot]
        ga_ref[block_of(slot)] = (value * live(slot)).astype(BF16)
    ga_ref[BLOCKS - 1] = jnp.zeros((SPLIT, thin, heads), BF16)

    @pl.loop(0, heads // tile)
    def _(j):
        at = pl.ds(pl.multiple_of(j * tile, tile), tile)
        gw_ref[at, :] = (total[at, :] * scale).astype(BF16)

    @pl.loop(1, n)
    def _(k):
        gp_copy(lax.rem(d + k, n), d).wait_send()
        for r in range(1, PIECES):
            share_copy(lax.rem(d + k, n), r, piece_of(2) if r == 3 else q).wait_send()

    @pl.loop(0, steps)
    def _(step):
        @pl.when(d < n - 1)
        def _():
            chain_copy(step, up_out.at[step], up_in, up_send, up_recv, lax.rem(d + 1, n)).wait_send()

        @pl.when(d > 0)
        def _():
            chain_copy(step, dn_out.at[step], dn_in, dn_send, dn_recv, lax.rem(d + n - 1, n)).wait_send()


def per_device(upstream, attn, gate, visible, proj_weight):
    slots, width = upstream.shape
    heads, cols = proj_weight.shape
    n = lax.axis_size("dp")
    rows = BLOCK // PIECES
    steps = n // 2 * BLOCKS * SPLIT
    thin = BLOCK // SPLIT
    scale = float(1.0 / np.sqrt(np.float32(slots * n)))
    any_space = pl.BlockSpec(memory_space=pl.ANY)
    in_vmem = pl.BlockSpec(memory_space=pltpu.VMEM)
    dma = pltpu.SemaphoreType.DMA
    grad_attn, grad_weight = pl.pallas_call(
        functools.partial(kernel, n, scale),
        out_shape=(
            jax.ShapeDtypeStruct((BLOCKS, SPLIT, thin, heads), BF16),
            jax.ShapeDtypeStruct((heads, cols), BF16),
        ),
        in_specs=[any_space, any_space, in_vmem, pl.BlockSpec(memory_space=pltpu.SMEM), any_space],
        out_specs=(in_vmem, in_vmem),
        scratch_shapes=[
            pltpu.VMEM((LIVE, rows, width), BF16),
            pltpu.VMEM((LIVE, PIECES, rows, cols), BF16),
            pltpu.VMEM((BLOCKS, SPLIT, thin, heads), BF16),
            pltpu.VMEM((heads, cols), BF16),
            pltpu.VMEM((n, LIVE, rows, cols), BF16),
            pltpu.VMEM((n, LIVE, PIECES, rows, cols), BF16),
            pltpu.VMEM((n, BLOCKS, SPLIT, thin, heads), F32),
            pltpu.VMEM((heads, cols), F32),
            pltpu.VMEM((steps, thin, heads), BF16),
            pltpu.VMEM((steps, thin, heads), BF16),
            pltpu.VMEM((steps, thin, heads), BF16),
            pltpu.VMEM((steps, thin, heads), BF16),
            dma((2 * LIVE + 1 + BLOCKS,)),
            dma((n,)), dma((n,)),
            dma((n, PIECES - 1)), dma((n, PIECES - 1)),
            dma((steps,)), dma((steps,)), dma((steps,)), dma((steps,)),
        ],
        compiler_params=pltpu.CompilerParams(
            collective_id=0, has_side_effects=True, vmem_limit_bytes=56 * 1024 * 1024
        ),
    )(
        upstream.reshape(BLOCKS, PIECES, rows, width),
        attn.reshape(BLOCKS, SPLIT, thin, heads),
        gate,
        visible,
        proj_weight,
    )
    return grad_attn.reshape(slots, heads), grad_weight


def solution(mesh):
    return jax.shard_map(
        per_device,
        mesh=mesh,
        in_specs=(
            P(("groups", "dp"), None),
            P(("groups", "dp"), ("mp", "sub")),
            P(("groups", "dp"), None),
            P(("groups", "dp")),
            P(("mp", "sub"), "dp"),
        ),
        out_specs=(P(("groups", "dp"), ("mp", "sub")), P(("mp", "sub"), ("groups", "dp"))),
        check_vma=False,
    )
```
